1024 devices in a mesh: shard: 8 (over x, core), narrow: 4 (over y), wide: 32 (over z).
Axes of the slice: x: 4, y: 4, z: 32, core: 2. Of those that a mesh axis runs over, the one named last changes fastest.
Arguments:
- tokens: bfloat16 [8192, 4096], P(('narrow', 'wide'), 'shard'), may hold values from -6 to 6
- routes: int32 [8192, 8], P(('narrow', 'wide')), may hold values from 0 to 127, all different within a row; in each aligned block of 64 rows (0 to 63, 64 to 127, ...) at most 8 rows name the same one
- route_weight: float32 [8192, 8], P(('narrow', 'wide')), may hold values from 0.1 to 1
- gate_weight: bfloat16 [128, 4096, 1024], P(('narrow', 'wide'), None, 'shard'), may hold values from -0.09375 to 0.09375
- up_weight: bfloat16 [128, 4096, 1024], P(('narrow', 'wide'), None, 'shard'), may hold values from -0.09375 to 0.09375
- down_weight: bfloat16 [128, 1024, 4096], P(('narrow', 'wide'), 'shard'), may hold values from -0.1875 to 0.1875
Outputs:
- mixed: bfloat16 [8192, 4096], P(('narrow', 'wide'), 'shard')
The draws below stay inside these ranges and needn't reach their ends.
Inputs may be any that keep to these rules, and one draw needn't show every extreme that they name: `routes`: within the 64 rows of one index of narrow and wide, no expert is named more than 8 times; each row names 8 different experts.
All inputs are finite; a program needn't handle non-finite values.
Results may differ from the reference program's by a relative error of at most 0.02.
Values may be sent and summed in bfloat16 or wider, within the bound.
No kernel may reach another device: no remote copies, remote signals or barrier semaphores. Data moves between devices by JAX's collectives and lax.ppermute only.
A program may use at most 64 MiB of HBM per device.

```python
import math
import jax
import jax.numpy as jnp
import numpy as np
from jax import lax

D = 4096
TOP = 8
FF = 1024
TOK_DEV = 64
EXPERTS = 128
CAP = 8
TOKENS = 8192
N_SHARD = 8


def shard_levels(rng, shape, pieces, least, largest):
    def one(position, shards_of):
        steps = jax.random.uniform(jax.random.fold_in(jax.random.fold_in(rng, 6), position), (shards_of,), jnp.float32, least / len(pieces), largest / len(pieces))
        return jnp.repeat(jnp.exp(steps), shape[position] // shards_of).reshape((-1,) + (1,) * (len(shape) - position - 1))

    gain = one(*pieces[0])
    for cut in pieces[1:]:
        gain = gain * one(*cut)
    return gain


def shared_out(stream_key, own, number, rows, count, top, most, slope):
    ranking = jax.random.permutation(stream_key, count)
    crowded, common = portions_of(count, rows * top, most, slope, True), portions_of(count, rows * top, most, slope, False)
    places = jnp.arange(count)

    def named(sizes, rotation):
        used = int((sizes > 0).sum())
        fixed = max(1, used // 4)
        moved = fixed + (places - fixed + rotation * (used - fixed)) % max(1, count - fixed)
        return jnp.zeros((count,), jnp.int32).at[ranking[jnp.where(places < fixed, places, moved)]].set(jnp.asarray(sizes, jnp.int32))

    sizes = jnp.where(number % 4 == 0, named(crowded, number // 4), named(common, number - number // 4 - 1))
    mixed = jax.random.permutation(jax.random.fold_in(own, 3), count)
    source_of, sink = mixed[0:count // 2 * 2:2], mixed[1:count // 2 * 2:2]
    slack = jnp.minimum(sizes[source_of] - 1, most - sizes[sink]) // 2
    slack = jnp.where((source_of == ranking[0]) | (sink == ranking[0]) | (sizes[sink] == 0), 0, jnp.maximum(slack, 0))
    moved = jax.random.randint(jax.random.fold_in(own, 4), (count // 2,), 0, 1 << 20) % (slack + 1)
    sizes = sizes.at[source_of].add(-moved).at[sink].add(moved)
    members = jnp.searchsorted(jnp.cumsum(sizes), jnp.arange(rows * top), side="right").astype(jnp.int32)
    listing = members.reshape(top, rows).T
    listing = listing[jax.random.permutation(jax.random.fold_in(own, 1), rows)]
    rotation = jax.random.randint(jax.random.fold_in(own, 2), (rows, 1), 0, top)
    return jnp.take_along_axis(listing, (jnp.arange(top)[None, :] + rotation) % top, axis=1)


def portions_of(count, total, bound, slope, full):
    loads = [(1 << 20) // math.isqrt(standing ** slope) + 1 for standing in range(1, count + 1)]
    largest = bound if full else min(bound, max(-(-total // count), total * loads[0] // sum(loads)))
    least = 1 if total - largest >= count - 1 else 0
    counts, surplus = [largest] + [least] * (count - 1), total - largest - least * (count - 1)
    while surplus > 0:
        candidates = [i for i in range(1, count) if counts[i] < largest] or [i for i in range(1, count) if counts[i] < bound]
        mass, budget = sum([loads[i] for i in candidates]), surplus
        for i in candidates:
            addition = min(bound - counts[i], max(1, budget * loads[i] // mass), surplus)
            counts[i] = counts[i] + addition
            surplus = surplus - addition
    return np.array(counts)


def noise(own_key, shape, deviation, bound, cuts=(), kind=jnp.bfloat16):
    drawn = jax.random.normal(own_key, shape, jnp.float32) * deviation
    if len(cuts) > 0:
        drawn = shard_levels(own_key, shape, cuts, -0.22, 0.18) * drawn
    return jnp.clip(drawn, min=-bound, max=bound).astype(kind)


def setup_inputs(seed: int = 0) -> dict:
    keys = jax.random.split(jax.random.key(seed), 7)
    tokens = noise(keys[0], (TOKENS, D), 1.0, 6.0, ((0, 128), (1, 8)))
    routes_keys = jax.random.split(jax.random.fold_in(keys[1], 1), TOKENS // TOK_DEV)
    routes_turns = jax.random.permutation(jax.random.fold_in(keys[1], 3), TOKENS // TOK_DEV)
    routes = jax.vmap(lambda own, number: shared_out(jax.random.fold_in(keys[1], 2), own, number, TOK_DEV, EXPERTS, TOP, CAP, 2))(routes_keys, routes_turns).reshape((TOKENS, TOP))
    route_weight = jnp.clip(0.1 + 0.9 * jax.random.uniform(keys[2], (TOKENS, TOP), jnp.float32) ** shard_levels(keys[2], (TOKENS, TOP), ((0, 128),), -0.2, 0.2), 0.1, 1.0)
    gate_weight = noise(keys[3], (EXPERTS, D, FF), D ** -0.5, 0.09375, ((0, 128), (2, 8)))
    up_weight = noise(keys[4], (EXPERTS, D, FF), D ** -0.5, 0.09375, ((0, 128), (2, 8)))
    down_weight = noise(keys[5], (EXPERTS, FF, D), FF ** -0.5, 0.1875, ((0, 128), (1, 8)))
    return dict(tokens=tokens, routes=routes, route_weight=route_weight, gate_weight=gate_weight, up_weight=up_weight, down_weight=down_weight)


def reference(tokens, routes, route_weight, gate_weight, up_weight, down_weight):
    groups = TOKENS // TOK_DEV
    flat_ids = routes.reshape(groups, TOK_DEV * TOP)
    onehot = (flat_ids[:, :, None] == jnp.arange(EXPERTS, dtype=jnp.int32)[None, None, :]).astype(jnp.int32)
    earlier = jnp.cumsum(onehot, axis=1) - onehot
    slot_rank = jnp.sum(earlier * onehot, axis=2)
    group_of = jnp.arange(groups, dtype=jnp.int32)[:, None]
    target = ((flat_ids * groups + group_of) * CAP + slot_rank).reshape(-1).astype(jnp.int32)
    token_of = (jnp.arange(TOKENS * TOP, dtype=jnp.int32) // TOP).astype(jnp.int32)
    buffer = jnp.zeros((EXPERTS * groups * CAP, D), jnp.bfloat16).at[target].set(tokens[token_of])
    buffer = buffer.reshape(EXPERTS, groups * CAP, D)
    piece_width = FF // N_SHARD

    def expert(operands):
        expert_rows, gate_w, up_w, down_w = operands
        gate = jnp.dot(expert_rows, gate_w, preferred_element_type=jnp.float32)
        up = jnp.dot(expert_rows, up_w, preferred_element_type=jnp.float32)
        hidden = (jax.nn.silu(gate) * up).astype(jnp.bfloat16)
        running = jnp.zeros((expert_rows.shape[0], D), jnp.float32)
        for part_index in range(N_SHARD):
            lower = part_index * piece_width
            piece_term = jnp.dot(hidden[:, lower:lower + piece_width], down_w[lower:lower + piece_width], preferred_element_type=jnp.float32).astype(jnp.bfloat16)
            piece_term = lax.optimization_barrier(piece_term)
            running = running + piece_term.astype(jnp.float32)
        return running.astype(jnp.bfloat16)

    outputs = lax.map(expert, (buffer, gate_weight, up_weight, down_weight))
    picked = outputs.reshape(-1, D)[target]
    weighted = picked.astype(jnp.float32) * route_weight.reshape(-1)[:, None]
    mixed = jnp.sum(weighted.reshape(TOKENS, TOP, D), axis=1)
    return mixed.astype(jnp.bfloat16)
```

```python
import jax
import jax.numpy as jnp
from jax import lax
from jax.experimental import pallas as pl
from jax.experimental.pallas import tpu as pltpu
from jax.sharding import Mesh, PartitionSpec as P

BF = jnp.bfloat16
F32 = jnp.float32
CAP = 8
LOW = 4
VMEM = 56 << 20


def hits(meta, base, n_low, wide_count, n_rows):
    top = meta.shape[0] // 2
    tokens = 64
    row = lax.broadcasted_iota(jnp.int32, (n_rows, tokens), 0)
    slot = row % CAP
    place = row // CAP
    expert = ((place // n_low) * wide_count + place % n_low + base).astype(F32)
    hit = jnp.zeros((n_rows, tokens), F32)
    weight = jnp.zeros((n_rows, tokens), F32)
    for k in range(top):
        same = meta[k : k + 1, :tokens] == expert
        hit = jnp.where(same, 1.0, hit)
        weight = jnp.where(same, meta[top + k : top + k + 1, :tokens], weight)
    earlier = (
        lax.broadcasted_iota(jnp.int32, (tokens, tokens), 0)
        < lax.broadcasted_iota(jnp.int32, (tokens, tokens), 1)
    ).astype(BF)
    rank = jnp.dot(hit.astype(BF), earlier, preferred_element_type=F32)
    chosen = jnp.where(rank == slot.astype(F32), hit, 0.0)
    return chosen, chosen * weight


def select_kernel(n_low, wide_count, base_ref, x_ref, rows_ref):
    tokens = 64
    meta = x_ref[0, tokens:, :].astype(F32)
    chosen, _ = hits(meta, base_ref[0], n_low, wide_count, rows_ref.shape[1])
    rows_ref[0] = jnp.dot(
        chosen.astype(BF), x_ref[0, :tokens, :], preferred_element_type=F32
    ).astype(BF)


def combine_kernel(n_low, wide_count, base_ref, x_ref, back_ref, part_ref):
    meta = x_ref[0].astype(F32)
    _, weight = hits(meta, base_ref[0], n_low, wide_count, back_ref.shape[1])
    part_ref[0] = lax.dot_general(
        weight.astype(BF), back_ref[0], (((0,), (0,)), ((), ())), preferred_element_type=F32
    ).astype(BF)


def expert_kernel(x_ref, w_ref, out_ref, total):
    step = pl.program_id(0)
    pieces, _, piece = x_ref.shape
    d_model = pieces * piece
    ff = w_ref.shape[2] // 2

    both = jnp.zeros((x_ref.shape[1], 2 * ff), F32)
    for s in range(pieces):
        both += jnp.dot(
            x_ref[s], w_ref[0, s * piece : (s + 1) * piece, :], preferred_element_type=F32
        )
    gate, up = both[:, :ff], both[:, ff:]
    hidden = (gate / (1.0 + jnp.exp(-gate)) * up).astype(BF)
    width = w_ref.shape[2]
    for n in range(d_model // width):
        at = d_model + n * ff
        term = jnp.dot(hidden, w_ref[0, at : at + ff, :], preferred_element_type=F32)

        @pl.when(step == 0)
        def _():
            total[:, n * width : (n + 1) * width] = term

        @pl.when(step > 0)
        def _():
            total[:, n * width : (n + 1) * width] += term

    @pl.when(step == pl.num_programs(0) - 1)
    def _():
        for s in range(pieces):
            out_ref[s] = total[:, s * piece : (s + 1) * piece].astype(BF)


def sum_kernel(x_ref, out_ref):
    total = x_ref[0].astype(F32)
    for i in range(1, x_ref.shape[0]):
        total += x_ref[i].astype(F32)
    out_ref[...] = total.astype(BF)


def shards(tokens, routes, route_weight, gate_weight, up_weight, down_weight):
    n_shard, n_narrow = lax.axis_size("shard"), lax.axis_size("narrow")
    n_high, n_low = lax.axis_size("high"), lax.axis_size("low")
    wide_count = n_high * n_low
    token_count, piece = tokens.shape
    top = routes.shape[1]
    d_model, ff = gate_weight.shape[1:]
    slots = n_narrow * n_low * CAP
    params = pltpu.CompilerParams(vmem_limit_bytes=VMEM)
    smem = pl.BlockSpec(memory_space=pltpu.SMEM)

    packed = jnp.concatenate(
        [
            jnp.concatenate([gate_weight[0], up_weight[0]], axis=1),
            down_weight[0]
            .reshape(ff, d_model // (2 * ff), 2 * ff)
            .transpose(1, 0, 2)
            .reshape(d_model // 2, 2 * ff),
        ],
        axis=0,
    )
    weights = lax.all_gather(packed, "shard", axis=0, tiled=False)

    meta = jnp.concatenate([routes.T.astype(BF), route_weight.T.astype(BF)], axis=0)
    meta = jnp.pad(meta, ((0, 0), (0, piece - token_count)))
    near = lax.all_gather(
        jnp.concatenate([tokens, meta], axis=0), "high", axis=0, tiled=False
    )
    base = (lax.axis_index("high") * n_low).reshape(1).astype(jnp.int32)
    full = near.shape[1]
    rows = pl.pallas_call(
        lambda *refs: select_kernel(n_low, wide_count, *refs),
        grid=(n_high,),
        in_specs=[smem, pl.BlockSpec((1, full, piece), lambda h: (h, 0, 0))],
        out_specs=pl.BlockSpec((1, slots, piece), lambda h: (h, 0, 0)),
        out_shape=jax.ShapeDtypeStruct((n_high, slots, piece), BF),
        compiler_params=params,
        name="select",
    )(base, near)
    peers = ("shard", "narrow", "low")
    arrived = lax.all_to_all(
        rows.reshape(-1, CAP, piece), peers, split_axis=0, concat_axis=0, tiled=True
    ).reshape(n_shard, slots, piece)
    out = pl.pallas_call(
        expert_kernel,
        grid=(n_shard,),
        in_specs=[
            pl.BlockSpec(arrived.shape, lambda j: (0, 0, 0)),
            pl.BlockSpec((1,) + packed.shape, lambda j: (j, 0, 0)),
        ],
        out_specs=pl.BlockSpec(arrived.shape, lambda j: (0, 0, 0)),
        out_shape=jax.ShapeDtypeStruct(arrived.shape, BF),
        scratch_shapes=[pltpu.VMEM((slots, d_model), F32)],
        compiler_params=params,
        name="expert",
    )(arrived, weights)
    back = lax.all_to_all(
        out.reshape(-1, CAP, piece), peers, split_axis=0, concat_axis=0, tiled=True
    ).reshape(n_high, slots, piece)
    part = pl.pallas_call(
        lambda *refs: combine_kernel(n_low, wide_count, *refs),
        grid=(n_high,),
        in_specs=[
            smem,
            pl.BlockSpec((1, 2 * top, piece), lambda h: (h, token_count // (2 * top), 0)),
            pl.BlockSpec((1, slots, piece), lambda h: (h, 0, 0)),
        ],
        out_specs=pl.BlockSpec((1, token_count, piece), lambda h: (h, 0, 0)),
        out_shape=jax.ShapeDtypeStruct((n_high, token_count, piece), BF),
        compiler_params=params,
        name="combine",
    )(base, near, back)
    parts = lax.all_to_all(part, "high", split_axis=0, concat_axis=0, tiled=True)
    return pl.pallas_call(
        sum_kernel,
        out_shape=jax.ShapeDtypeStruct((token_count, piece), BF),
        compiler_params=params,
        name="sum",
    )(parts)


def solution(mesh):
    sizes = dict(mesh.shape)
    split = Mesh(
        mesh.devices.reshape(
            sizes["shard"], sizes["narrow"], sizes["wide"] // LOW, LOW
        ),
        ("shard", "narrow", "high", "low"),
    )
    group = ("narrow", "high", "low")
    placed = (
        P(group, "shard"),
        P(group, None),
        P(group, None),
        P(group, None, "shard"),
        P(group, None, "shard"),
        P(group, "shard", None),
    )
    return jax.shard_map(
        shards,
        mesh=split,
        in_specs=placed,
        out_specs=P(group, "shard"),
        check_vma=False,
    )
```

```python
import jax
import jax.numpy as jnp
from jax import lax
from jax.experimental import pallas as pl
from jax.experimental.pallas import tpu as pltpu
from jax.sharding import Mesh, PartitionSpec as P

BF = jnp.bfloat16
F32 = jnp.float32
CAP = 8
LOW = 4
VMEM = 56 << 20


def select_kernel(n_low, wide_count, base_ref, x_ref, rows_ref, weight_ref):
    pair, full, _ = x_ref.shape
    slots, lanes = weight_ref.shape[1:]
    tokens = lanes // pair
    top = (full - tokens) // 2
    meta = x_ref[0, tokens:, :lanes].astype(F32)
    for i in range(1, pair):
        meta += x_ref[i, tokens:, :lanes].astype(F32)
    row = lax.broadcasted_iota(jnp.int32, (slots, lanes), 0)
    lane = lax.broadcasted_iota(jnp.int32, (slots, lanes), 1)
    slot = row % CAP
    place = row // (CAP * pair)
    expert = ((place // n_low) * wide_count + place % n_low + base_ref[0]).astype(F32)
    expert = jnp.where(lane // tokens == (row // CAP) % pair, expert, -1.0)
    hit = jnp.zeros((slots, lanes), F32)
    weight = jnp.zeros((slots, lanes), F32)
    for k in range(top):
        same = meta[k : k + 1, :] == expert
        hit = jnp.where(same, 1.0, hit)
        weight = jnp.where(same, meta[top + k : top + k + 1, :], weight)
    earlier = (
        lax.broadcasted_iota(jnp.int32, (lanes, lanes), 0)
        < lax.broadcasted_iota(jnp.int32, (lanes, lanes), 1)
    ).astype(BF)
    rank = jnp.dot(hit.astype(BF), earlier, preferred_element_type=F32)
    first = rank == slot.astype(F32)
    chosen = jnp.where(first, hit, 0.0).astype(BF)
    weight_ref[0] = jnp.where(first, weight, 0.0).astype(BF)
    both = jnp.concatenate([x_ref[i, :tokens, :] for i in range(pair)], axis=0)
    rows_ref[0] = jnp.dot(chosen, both, preferred_element_type=F32).astype(BF)


def combine_kernel(weight_ref, back_ref, part_ref):
    part_ref[0] = lax.dot_general(
        weight_ref[0], back_ref[0], (((0,), (0,)), ((), ())), preferred_element_type=F32
    ).astype(BF)


def expert_kernel(
    core_ref, own_x, other_x, all_w, keep_ref, send_ref, weights, rows, hidden, total, sems
):
    n_x, n_rows, piece = own_x.shape
    d_model = rows.shape[1]
    width = weights.shape[2]
    ff = width // 2
    core = core_ref[0]
    copies = [
        pltpu.make_async_copy(all_w.at[b], weights.at[b], sems.at[b]) for b in range(n_x)
    ]
    for copy in copies:
        copy.start()
    for x in range(n_x):
        at = pl.multiple_of((2 * x + core) * piece, piece)
        rows[:, pl.ds(at, piece)] = own_x[x]
        at = pl.multiple_of((2 * x + 1 - core) * piece, piece)
        rows[:, pl.ds(at, piece)] = other_x[x]
    for b, copy in enumerate(copies):
        copy.wait()
        both = jnp.dot(rows[...], weights[b, :d_model, :], preferred_element_type=F32)
        gate, up = both[:, :ff], both[:, ff:]
        hidden[:, b * ff : (b + 1) * ff] = (gate / (1.0 + jnp.exp(-gate)) * up).astype(BF)
    for n in range(d_model // width):
        at = d_model + n * ff
        down = jnp.concatenate(
            [weights[b, at : at + ff, :] for b in range(len(copies))], axis=0
        )
        total[:, n * width : (n + 1) * width] = jnp.dot(
            hidden[...], down, preferred_element_type=F32
        ).astype(BF)
    for x in range(n_x):
        at = pl.multiple_of((2 * x + core) * piece, piece)
        keep_ref[x] = total[:, pl.ds(at, piece)]
        at = pl.multiple_of((2 * x + 1 - core) * piece, piece)
        send_ref[x] = total[:, pl.ds(at, piece)]


def shards(tokens, routes, route_weight, gate_weight, up_weight, down_weight):
    n_x, n_narrow = lax.axis_size("x"), lax.axis_size("narrow")
    n_high, n_low = lax.axis_size("high"), lax.axis_size("low")
    token_count, piece = tokens.shape
    d_model, ff = gate_weight.shape[1:]
    pair = n_high // n_x
    lanes = pair * token_count
    slots = n_narrow * n_low * pair * CAP
    params = pltpu.CompilerParams(vmem_limit_bytes=VMEM)
    smem = pl.BlockSpec(memory_space=pltpu.SMEM)
    vmem = pl.BlockSpec(memory_space=pltpu.VMEM)
    hbm = pl.BlockSpec(memory_space=pl.ANY)
    swap = [(0, 1), (1, 0)]

    own_w = jnp.concatenate(
        [
            jnp.concatenate([gate_weight[0], up_weight[0]], axis=1),
            down_weight[0]
            .reshape(ff, d_model // (2 * ff), 2 * ff)
            .transpose(1, 0, 2)
            .reshape(d_model // 2, 2 * ff),
        ],
        axis=0,
    )
    all_w = lax.all_gather(own_w, "x", axis=0, tiled=False)

    high = lax.axis_index("high")
    meta = jnp.concatenate([routes.T.astype(BF), route_weight.T.astype(BF)], axis=0)
    meta = jnp.tile(meta, (1, pair))
    mine = jnp.arange(lanes) // token_count == high % pair
    meta = jnp.where(mine[None, :], meta, jnp.zeros_like(meta))
    meta = jnp.pad(meta, ((0, 0), (0, piece - lanes)))
    near = lax.all_gather(
        jnp.concatenate([tokens, meta], axis=0), "high", axis=0, tiled=False
    )
    base = (high * n_low).reshape(1).astype(jnp.int32)
    core = lax.axis_index("core").reshape(1).astype(jnp.int32)
    full = near.shape[1]
    rows, weight = pl.pallas_call(
        lambda *refs: select_kernel(n_low, n_high * n_low, *refs),
        grid=(n_x,),
        in_specs=[smem, pl.BlockSpec((pair, full, piece), lambda h: (h, 0, 0))],
        out_specs=[
            pl.BlockSpec((1, slots, piece), lambda h: (h, 0, 0)),
            pl.BlockSpec((1, slots, lanes), lambda h: (h, 0, 0)),
        ],
        out_shape=[
            jax.ShapeDtypeStruct((n_x, slots, piece), BF),
            jax.ShapeDtypeStruct((n_x, slots, lanes), BF),
        ],
        compiler_params=params,
        name="select",
    )(base, near)
    peers = ("x", "narrow", "low")
    own_x = lax.all_to_all(
        rows.reshape(-1, pair * CAP, piece), peers, split_axis=0, concat_axis=0, tiled=True
    ).reshape(n_x, slots, piece)
    other_x = lax.ppermute(own_x, "core", swap)
    keep, send = pl.pallas_call(
        expert_kernel,
        in_specs=[smem, vmem, vmem, hbm],
        out_specs=[vmem, vmem],
        out_shape=[jax.ShapeDtypeStruct(own_x.shape, BF)] * 2,
        scratch_shapes=[
            pltpu.VMEM((n_x,) + own_w.shape, BF),
            pltpu.VMEM((slots, d_model), BF),
            pltpu.VMEM((slots, n_x * ff), BF),
            pltpu.VMEM((slots, d_model), BF),
            pltpu.SemaphoreType.DMA((n_x,)),
        ],
        compiler_params=params,
        name="expert",
    )(core, own_x, other_x, all_w)
    got = lax.ppermute(send, "core", swap)
    out = (keep.astype(F32) + got.astype(F32)).astype(BF)
    back = lax.all_to_all(
        out.reshape(-1, pair * CAP, piece), peers, split_axis=0, concat_axis=0, tiled=True
    ).reshape(n_x, slots, piece)
    part = pl.pallas_call(
        combine_kernel,
        grid=(n_x,),
        in_specs=[
            pl.BlockSpec((1, slots, lanes), lambda h: (h, 0, 0)),
            pl.BlockSpec((1, slots, piece), lambda h: (h, 0, 0)),
        ],
        out_specs=pl.BlockSpec((1, lanes, piece), lambda h: (h, 0, 0)),
        out_shape=jax.ShapeDtypeStruct((n_x, lanes, piece), BF),
        compiler_params=params,
        name="combine",
    )(weight, back)
    return lax.psum_scatter(
        part.reshape(n_high, token_count, piece), "high", scatter_dimension=0, tiled=False
    )


def solution(mesh):
    sizes = dict(mesh.shape)
    split = Mesh(
        mesh.devices.reshape(
            sizes["shard"] // 2, 2, sizes["narrow"], sizes["wide"] // LOW, LOW
        ),
        ("x", "core", "narrow", "high", "low"),
    )
    group, shard = ("narrow", "high", "low"), ("x", "core")
    placed = (
        P(group, shard),
        P(group, None),
        P(group, None),
        P(group, None, shard),
        P(group, None, shard),
        P(group, shard, None),
    )
    return jax.shard_map(
        shards,
        mesh=split,
        in_specs=placed,
        out_specs=P(group, shard),
        check_vma=False,
    )
```

```python
import jax
import jax.numpy as jnp
from jax import lax
from jax.experimental import pallas as pl
from jax.experimental.pallas import tpu as pltpu
from jax.sharding import Mesh, PartitionSpec as P

BF = jnp.bfloat16
F32 = jnp.float32
CAP = 8
LOW = 4
VMEM = 56 << 20


def select_kernel(n_low, wide_count, base_ref, x_ref, rows_ref, weight_ref):
    pair, full, _ = x_ref.shape
    slots, lanes = weight_ref.shape[1:]
    tokens = lanes // pair
    top = (full - tokens) // 2
    meta = x_ref[0, tokens:, :lanes].astype(F32)
    for i in range(1, pair):
        meta += x_ref[i, tokens:, :lanes].astype(F32)
    row = lax.broadcasted_iota(jnp.int32, (slots, lanes), 0)
    lane = lax.broadcasted_iota(jnp.int32, (slots, lanes), 1)
    slot = row % CAP
    place = row // (CAP * pair)
    expert = ((place // n_low) * wide_count + place % n_low + base_ref[0]).astype(F32)
    expert = jnp.where(lane // tokens == (row // CAP) % pair, expert, -1.0)
    hit = jnp.zeros((slots, lanes), F32)
    weight = jnp.zeros((slots, lanes), F32)
    for k in range(top):
        same = meta[k : k + 1, :] == expert
        hit = jnp.where(same, 1.0, hit)
        weight = jnp.where(same, meta[top + k : top + k + 1, :], weight)
    earlier = (
        lax.broadcasted_iota(jnp.int32, (lanes, lanes), 0)
        < lax.broadcasted_iota(jnp.int32, (lanes, lanes), 1)
    ).astype(BF)
    rank = jnp.dot(hit.astype(BF), earlier, preferred_element_type=F32)
    first = rank == slot.astype(F32)
    chosen = jnp.where(first, hit, 0.0).astype(BF)
    weight_ref[0] = jnp.where(first, weight, 0.0).astype(BF)
    both = jnp.concatenate([x_ref[i, :tokens, :] for i in range(pair)], axis=0)
    rows_ref[0] = jnp.dot(chosen, both, preferred_element_type=F32).astype(BF)


def combine_kernel(weight_ref, back_ref, part_ref):
    part_ref[0] = lax.dot_general(
        weight_ref[0], back_ref[0], (((0,), (0,)), ((), ())), preferred_element_type=F32
    ).astype(BF)


def expert_kernel(
    core_ref, own_x, other_x, *refs
):
    parts, (keep_ref, send_ref, weights, rows, hidden, total, sems) = refs[:-7], refs[-7:]
    n_x, n_rows, piece = own_x.shape
    d_model = rows.shape[1]
    width = weights.shape[2]
    ff = width // 2
    core = core_ref[0]
    half = parts[0].shape[0]
    copies = [
        pltpu.make_async_copy(
            part, weights.at[i // 2, (i % 2) * half : (i % 2 + 1) * half], sems.at[i]
        )
        for i, part in enumerate(parts)
    ]
    for copy in copies:
        copy.start()
    for x in range(n_x):
        at = pl.multiple_of((2 * x + core) * piece, piece)
        rows[:, pl.ds(at, piece)] = own_x[x]
        at = pl.multiple_of((2 * x + 1 - core) * piece, piece)
        rows[:, pl.ds(at, piece)] = other_x[x]
    for b in range(n_x):
        copies[2 * b].wait()
        copies[2 * b + 1].wait()
        both = jnp.dot(rows[...], weights[b, :d_model, :], preferred_element_type=F32)
        gate, up = both[:, :ff], both[:, ff:]
        hidden[:, b * ff : (b + 1) * ff] = (gate / (1.0 + jnp.exp(-gate)) * up).astype(BF)
    for n in range(d_model // width):
        at = d_model + n * ff
        down = jnp.concatenate(
            [weights[b, at : at + ff, :] for b in range(n_x)], axis=0
        )
        total[:, n * width : (n + 1) * width] = jnp.dot(
            hidden[...], down, preferred_element_type=F32
        ).astype(BF)
    for x in range(n_x):
        at = pl.multiple_of((2 * x + core) * piece, piece)
        keep_ref[x] = total[:, pl.ds(at, piece)]
        at = pl.multiple_of((2 * x + 1 - core) * piece, piece)
        send_ref[x] = total[:, pl.ds(at, piece)]


def shards(tokens, routes, route_weight, gate_weight, up_weight, down_weight):
    n_x, n_narrow = lax.axis_size("x"), lax.axis_size("narrow")
    n_high, n_low = lax.axis_size("high"), lax.axis_size("low")
    token_count, piece = tokens.shape
    d_model, ff = gate_weight.shape[1:]
    pair = n_high // n_x
    lanes = pair * token_count
    slots = n_narrow * n_low * pair * CAP
    params = pltpu.CompilerParams(vmem_limit_bytes=VMEM)
    smem = pl.BlockSpec(memory_space=pltpu.SMEM)
    vmem = pl.BlockSpec(memory_space=pltpu.VMEM)
    hbm = pl.BlockSpec(memory_space=pl.ANY)
    swap = [(0, 1), (1, 0)]
    up_x = [(i, (i + 1) % n_x) for i in range(n_x)]
    down_x = [(i, (i - 1) % n_x) for i in range(n_x)]

    own_w = jnp.concatenate(
        [
            jnp.concatenate([gate_weight[0], up_weight[0]], axis=1),
            down_weight[0]
            .reshape(ff, d_model // (2 * ff), 2 * ff)
            .transpose(1, 0, 2)
            .reshape(d_model // 2, 2 * ff),
        ],
        axis=0,
    )
    half = own_w.shape[0] // 2
    own_a, own_b = own_w[:half], own_w[half:]
    prev_a = lax.ppermute(own_a, "x", up_x)
    next_b = lax.ppermute(own_b, "x", down_x)
    prev_b = lax.ppermute(own_b, "x", up_x)
    next_a = lax.ppermute(own_a, "x", down_x)

    high = lax.axis_index("high")
    meta = jnp.concatenate([routes.T.astype(BF), route_weight.T.astype(BF)], axis=0)
    meta = jnp.tile(meta, (1, pair))
    mine = jnp.arange(lanes) // token_count == high % pair
    meta = jnp.where(mine[None, :], meta, jnp.zeros_like(meta))
    meta = jnp.pad(meta, ((0, 0), (0, piece - lanes)))
    near = lax.all_gather(
        jnp.concatenate([tokens, meta], axis=0), "high", axis=0, tiled=False
    )
    near, prev_a, next_b = lax.optimization_barrier((near, prev_a, next_b))
    far_a = lax.ppermute(prev_a, "x", up_x)
    far_b = lax.ppermute(next_b, "x", down_x)
    base = (high * n_low).reshape(1).astype(jnp.int32)
    core = lax.axis_index("core").reshape(1).astype(jnp.int32)
    full = near.shape[1]
    rows, weight = pl.pallas_call(
        lambda *refs: select_kernel(n_low, n_high * n_low, *refs),
        grid=(n_x,),
        in_specs=[smem, pl.BlockSpec((pair, full, piece), lambda h: (h, 0, 0))],
        out_specs=[
            pl.BlockSpec((1, slots, piece), lambda h: (h, 0, 0)),
            pl.BlockSpec((1, slots, lanes), lambda h: (h, 0, 0)),
        ],
        out_shape=[
            jax.ShapeDtypeStruct((n_x, slots, piece), BF),
            jax.ShapeDtypeStruct((n_x, slots, lanes), BF),
        ],
        compiler_params=params,
        name="select",
    )(base, near)
    rows, prev_b, next_a = lax.optimization_barrier((rows, prev_b, next_a))
    peers = ("x", "narrow", "low")
    own_x = lax.all_to_all(
        rows.reshape(-1, pair * CAP, piece), peers, split_axis=0, concat_axis=0, tiled=True
    ).reshape(n_x, slots, piece)
    other_x = lax.ppermute(own_x, "core", swap)
    keep, send = pl.pallas_call(
        expert_kernel,
        in_specs=[smem, vmem, vmem] + [hbm] * (2 * n_x),
        out_specs=[vmem, vmem],
        out_shape=[jax.ShapeDtypeStruct(own_x.shape, BF)] * 2,
        scratch_shapes=[
            pltpu.VMEM((n_x,) + own_w.shape, BF),
            pltpu.VMEM((slots, d_model), BF),
            pltpu.VMEM((slots, n_x * ff), BF),
            pltpu.VMEM((slots, d_model), BF),
            pltpu.SemaphoreType.DMA((2 * n_x,)),
        ],
        compiler_params=params,
        name="expert",
    )(core, own_x, other_x, own_a, own_b, prev_a, prev_b, next_a, next_b, far_a, far_b)
    got = lax.ppermute(send, "core", swap)
    out = (keep.astype(F32) + got.astype(F32)).astype(BF)
    back = lax.all_to_all(
        out.reshape(-1, pair * CAP, piece), peers, split_axis=0, concat_axis=0, tiled=True
    ).reshape(n_x, slots, piece)
    part = pl.pallas_call(
        combine_kernel,
        grid=(n_x,),
        in_specs=[
            pl.BlockSpec((1, slots, lanes), lambda h: (h, 0, 0)),
            pl.BlockSpec((1, slots, piece), lambda h: (h, 0, 0)),
        ],
        out_specs=pl.BlockSpec((1, lanes, piece), lambda h: (h, 0, 0)),
        out_shape=jax.ShapeDtypeStruct((n_x, lanes, piece), BF),
        compiler_params=params,
        name="combine",
    )(weight, back)
    return lax.psum_scatter(
        part.reshape(n_high, token_count, piece), "high", scatter_dimension=0, tiled=False
    )


def solution(mesh):
    sizes = dict(mesh.shape)
    split = Mesh(
        mesh.devices.reshape(
            sizes["shard"] // 2, 2, sizes["narrow"], sizes["wide"] // LOW, LOW
        ),
        ("x", "core", "narrow", "high", "low"),
    )
    group, shard = ("narrow", "high", "low"), ("x", "core")
    placed = (
        P(group, shard),
        P(group, None),
        P(group, None),
        P(group, None, shard),
        P(group, None, shard),
        P(group, shard, None),
    )
    return jax.shard_map(
        shards,
        mesh=split,
        in_specs=placed,
        out_specs=P(group, shard),
        check_vma=False,
    )
```

```python
import jax
import jax.numpy as jnp
from jax import lax
from jax.experimental import pallas as pl
from jax.experimental.pallas import tpu as pltpu
from jax.sharding import Mesh, PartitionSpec as P

BF = jnp.bfloat16
F32 = jnp.float32
CAP = 8
LOW = 4
VMEM = 56 << 20


def select_kernel(n_low, wide_count, base_ref, x_ref, rows_ref, weight_ref):
    pair, full, _ = x_ref.shape
    slots, lanes = weight_ref.shape[1:]
    tokens = lanes // pair
    top = (full - tokens) // 2
    meta = x_ref[0, tokens:, :lanes].astype(F32)
    for i in range(1, pair):
        meta += x_ref[i, tokens:, :lanes].astype(F32)
    row = lax.broadcasted_iota(jnp.int32, (slots, lanes), 0)
    lane = lax.broadcasted_iota(jnp.int32, (slots, lanes), 1)
    slot = row % CAP
    place = row // (CAP * pair)
    expert = ((place // n_low) * wide_count + place % n_low + base_ref[0]).astype(F32)
    expert = jnp.where(lane // tokens == (row // CAP) % pair, expert, -1.0)
    hit = jnp.zeros((slots, lanes), F32)
    weight = jnp.zeros((slots, lanes), F32)
    for k in range(top):
        same = meta[k : k + 1, :] == expert
        hit = jnp.where(same, 1.0, hit)
        weight = jnp.where(same, meta[top + k : top + k + 1, :], weight)
    earlier = (
        lax.broadcasted_iota(jnp.int32, (lanes, lanes), 0)
        < lax.broadcasted_iota(jnp.int32, (lanes, lanes), 1)
    ).astype(BF)
    rank = jnp.dot(hit.astype(BF), earlier, preferred_element_type=F32)
    first = rank == slot.astype(F32)
    chosen = jnp.where(first, hit, 0.0).astype(BF)
    weight_ref[0] = jnp.where(first, weight, 0.0).astype(BF)
    both = jnp.concatenate([x_ref[i, :tokens, :] for i in range(pair)], axis=0)
    rows_ref[0] = jnp.dot(chosen, both, preferred_element_type=F32).astype(BF)


def combine_kernel(weight_ref, back_ref, part_ref):
    part_ref[0] = lax.dot_general(
        weight_ref[0], back_ref[0], (((0,), (0,)), ((), ())), preferred_element_type=F32
    ).astype(BF)


def expert_kernel(
    core_ref, own_x, other_x, *refs
):
    parts, (keep_ref, send_ref, weights, rows, hidden, total, sems) = refs[:-7], refs[-7:]
    n_x, n_rows, piece = own_x.shape
    d_model = rows.shape[1]
    width = weights.shape[2]
    ff = width // 2
    core = core_ref[0]
    half = parts[0].shape[0]
    copies = [
        pltpu.make_async_copy(
            part, weights.at[i // 2, (i % 2) * half : (i % 2 + 1) * half], sems.at[i]
        )
        for i, part in enumerate(parts)
    ]
    for copy in copies:
        copy.start()
    for x in range(n_x):
        at = pl.multiple_of((2 * x + core) * piece, piece)
        rows[:, pl.ds(at, piece)] = own_x[x]
        at = pl.multiple_of((2 * x + 1 - core) * piece, piece)
        rows[:, pl.ds(at, piece)] = other_x[x]
    for b in range(n_x):
        copies[2 * b].wait()
        copies[2 * b + 1].wait()
        both = jnp.dot(rows[...], weights[b, :d_model, :], preferred_element_type=F32)
        gate, up = both[:, :ff], both[:, ff:]
        hidden[:, b * ff : (b + 1) * ff] = (gate / (1.0 + jnp.exp(-gate)) * up).astype(BF)
    for n in range(d_model // width):
        at = d_model + n * ff
        down = jnp.concatenate(
            [weights[b, at : at + ff, :] for b in range(n_x)], axis=0
        )
        total[:, n * width : (n + 1) * width] = jnp.dot(
            hidden[...], down, preferred_element_type=F32
        ).astype(BF)
    for x in range(n_x):
        at = pl.multiple_of((2 * x + core) * piece, piece)
        keep_ref[x] = total[:, pl.ds(at, piece)]
        at = pl.multiple_of((2 * x + 1 - core) * piece, piece)
        send_ref[x] = total[:, pl.ds(at, piece)]


def shards(tokens, routes, route_weight, gate_weight, up_weight, down_weight):
    n_x, n_narrow = lax.axis_size("x"), lax.axis_size("narrow")
    n_high, n_low = lax.axis_size("high"), lax.axis_size("low")
    token_count, piece = tokens.shape
    d_model, ff = gate_weight.shape[1:]
    pair = n_high // n_x
    lanes = pair * token_count
    slots = n_narrow * n_low * pair * CAP
    params = pltpu.CompilerParams(vmem_limit_bytes=VMEM)
    smem = pl.BlockSpec(memory_space=pltpu.SMEM)
    vmem = pl.BlockSpec(memory_space=pltpu.VMEM)
    hbm = pl.BlockSpec(memory_space=pl.ANY)
    swap = [(0, 1), (1, 0)]
    up_x = [(i, (i + 1) % n_x) for i in range(n_x)]
    down_x = [(i, (i - 1) % n_x) for i in range(n_x)]

    own_w = jnp.concatenate(
        [
            jnp.concatenate([gate_weight[0], up_weight[0]], axis=1),
            down_weight[0]
            .reshape(ff, d_model // (2 * ff), 2 * ff)
            .transpose(1, 0, 2)
            .reshape(d_model // 2, 2 * ff),
        ],
        axis=0,
    )
    half = own_w.shape[0] // 2
    own_a, own_b = own_w[:half], own_w[half:]
    prev_a = lax.ppermute(own_a, "x", up_x)
    next_b = lax.ppermute(own_b, "x", down_x)
    prev_b = lax.ppermute(own_b, "x", up_x)
    next_a = lax.ppermute(own_a, "x", down_x)

    high = lax.axis_index("high")
    meta = jnp.concatenate([routes.T.astype(BF), route_weight.T.astype(BF)], axis=0)
    meta = jnp.tile(meta, (1, pair))
    mine = jnp.arange(lanes) // token_count == high % pair
    meta = jnp.where(mine[None, :], meta, jnp.zeros_like(meta))
    meta = jnp.pad(meta, ((0, 0), (0, piece - lanes)))
    near = lax.all_gather(
        jnp.concatenate([tokens, meta], axis=0), "high", axis=0, tiled=False
    )
    near, prev_a, next_b = lax.optimization_barrier((near, prev_a, next_b))
    far_a = lax.ppermute(prev_a, "x", up_x)
    far_b = lax.ppermute(next_b, "x", down_x)
    base = (high * n_low).reshape(1).astype(jnp.int32)
    core = lax.axis_index("core").reshape(1).astype(jnp.int32)
    full = near.shape[1]
    rows, weight = pl.pallas_call(
        lambda *refs: select_kernel(n_low, n_high * n_low, *refs),
        grid=(n_x,),
        in_specs=[smem, pl.BlockSpec((pair, full, piece), lambda h: (h, 0, 0))],
        out_specs=[
            pl.BlockSpec((1, slots, piece), lambda h: (h, 0, 0)),
            pl.BlockSpec((1, slots, lanes), lambda h: (h, 0, 0)),
        ],
        out_shape=[
            jax.ShapeDtypeStruct((n_x, slots, piece), BF),
            jax.ShapeDtypeStruct((n_x, slots, lanes), BF),
        ],
        compiler_params=params,
        name="select",
    )(base, near)
    rows, prev_b, next_a = lax.optimization_barrier((rows, prev_b, next_a))
    peers = ("x", "narrow", "low")
    own_x = lax.all_to_all(
        rows.reshape(-1, pair * CAP, piece), peers, split_axis=0, concat_axis=0, tiled=True
    ).reshape(n_x, slots, piece)
    other_x = lax.ppermute(own_x, "core", swap)
    keep, send = pl.pallas_call(
        expert_kernel,
        in_specs=[smem, vmem, vmem] + [hbm] * (2 * n_x),
        out_specs=[vmem, vmem],
        out_shape=[jax.ShapeDtypeStruct(own_x.shape, BF)] * 2,
        scratch_shapes=[
            pltpu.VMEM((n_x,) + own_w.shape, BF),
            pltpu.VMEM((slots, d_model), BF),
            pltpu.VMEM((slots, n_x * ff), BF),
            pltpu.VMEM((slots, d_model), BF),
            pltpu.SemaphoreType.DMA((2 * n_x,)),
        ],
        compiler_params=params,
        name="expert",
    )(core, own_x, other_x, own_a, own_b, prev_a, prev_b, next_a, next_b, far_a, far_b)
    got = lax.ppermute(send, "core", swap)
    out = (keep.astype(F32) + got.astype(F32)).astype(BF)
    back = lax.all_to_all(
        out.reshape(-1, pair * CAP, piece), peers, split_axis=0, concat_axis=0, tiled=True
    ).reshape(n_x, slots, piece)
    part = pl.pallas_call(
        combine_kernel,
        grid=(n_x,),
        in_specs=[
            pl.BlockSpec((1, slots, lanes), lambda h: (h, 0, 0)),
            pl.BlockSpec((1, slots, piece), lambda h: (h, 0, 0)),
        ],
        out_specs=pl.BlockSpec((1, lanes, piece), lambda h: (h, 0, 0)),
        out_shape=jax.ShapeDtypeStruct((n_x, lanes, piece), BF),
        compiler_params=params,
        name="combine",
    )(weight, back)
    part = part.reshape(n_high, token_count, piece)
    up_z = [(i, (i + 1) % n_high) for i in range(n_high)]
    down_z = [(i, (i - 1) % n_high) for i in range(n_high)]

    def mine_for(step):
        block = lax.rem(high + step, n_high)
        return lax.dynamic_slice_in_dim(part, block, 1, 0)[0].astype(F32)

    reach = n_high // 2
    rising = lax.ppermute(mine_for(reach).astype(BF), "high", up_z)
    falling = lax.ppermute(mine_for(reach + 1).astype(BF), "high", down_z)
    for step in range(1, reach):
        rising = (rising.astype(F32) + mine_for(reach - step)).astype(BF)
        rising = lax.ppermute(rising, "high", up_z)
        if step < reach - 1:
            falling = (falling.astype(F32) + mine_for(reach + 1 + step)).astype(BF)
            falling = lax.ppermute(falling, "high", down_z)
    return (mine_for(0) + rising.astype(F32) + falling.astype(F32)).astype(BF)


def solution(mesh):
    sizes = dict(mesh.shape)
    split = Mesh(
        mesh.devices.reshape(
            sizes["shard"] // 2, 2, sizes["narrow"], sizes["wide"] // LOW, LOW
        ),
        ("x", "core", "narrow", "high", "low"),
    )
    group, shard = ("narrow", "high", "low"), ("x", "core")
    placed = (
        P(group, shard),
        P(group, None),
        P(group, None),
        P(group, None, shard),
        P(group, None, shard),
        P(group, shard, None),
    )
    return jax.shard_map(
        shards,
        mesh=split,
        in_specs=placed,
        out_specs=P(group, shard),
        check_vma=False,
    )
```

```python
import jax
import jax.numpy as jnp
from jax import lax
from jax.experimental import pallas as pl
from jax.experimental.pallas import tpu as pltpu
from jax.sharding import Mesh, PartitionSpec as P

BF = jnp.bfloat16
F32 = jnp.float32
CAP = 8
LOW = 4
VMEM = 56 << 20


def select_kernel(n_low, wide_count, base_ref, x_ref, rows_ref, weight_ref):
    pair, full, _ = x_ref.shape
    slots, lanes = weight_ref.shape[1:]
    tokens = lanes // pair
    top = (full - tokens) // 2
    meta = x_ref[0, tokens:, :lanes].astype(F32)
    for i in range(1, pair):
        meta += x_ref[i, tokens:, :lanes].astype(F32)
    row = lax.broadcasted_iota(jnp.int32, (slots, lanes), 0)
    lane = lax.broadcasted_iota(jnp.int32, (slots, lanes), 1)
    slot = row % CAP
    place = row // (CAP * pair)
    expert = ((place // n_low) * wide_count + place % n_low + base_ref[0]).astype(F32)
    expert = jnp.where(lane // tokens == (row // CAP) % pair, expert, -1.0)
    hit = jnp.zeros((slots, lanes), F32)
    weight = jnp.zeros((slots, lanes), F32)
    for k in range(top):
        same = meta[k : k + 1, :] == expert
        hit = jnp.where(same, 1.0, hit)
        weight = jnp.where(same, meta[top + k : top + k + 1, :], weight)
    earlier = (
        lax.broadcasted_iota(jnp.int32, (lanes, lanes), 0)
        < lax.broadcasted_iota(jnp.int32, (lanes, lanes), 1)
    ).astype(BF)
    rank = jnp.dot(hit.astype(BF), earlier, preferred_element_type=F32)
    first = rank == slot.astype(F32)
    chosen = jnp.where(first, hit, 0.0).astype(BF)
    weight_ref[0] = jnp.where(first, weight, 0.0).astype(BF)
    both = jnp.concatenate([x_ref[i, :tokens, :] for i in range(pair)], axis=0)
    rows_ref[0] = jnp.dot(chosen, both, preferred_element_type=F32).astype(BF)


def combine_kernel(weight_ref, back_ref, part_ref):
    back = back_ref[:, 0].reshape(weight_ref.shape[1], back_ref.shape[3])
    part_ref[0] = lax.dot_general(
        weight_ref[0], back, (((0,), (0,)), ((), ())), preferred_element_type=F32
    ).astype(BF)


def hidden_kernel(place_ref, own_x, other_x, *refs):
    parts, (out_ref, weights, rows, hidden, sems) = refs[:-5], refs[-5:]
    n_x, n_rows, piece = own_x.shape
    d_model = rows.shape[1]
    half = d_model // 2
    ff = weights.shape[2] // 2
    core, chip = place_ref[0], place_ref[1]
    copies = [
        pltpu.make_async_copy(
            part.at[:half], weights.at[i // 2, (i % 2) * half : (i % 2 + 1) * half], sems.at[i]
        )
        for i, part in enumerate(parts)
    ]
    for copy in copies:
        copy.start()
    for x in range(n_x):
        at = pl.multiple_of((2 * x + core) * piece, piece)
        rows[:, pl.ds(at, piece)] = own_x[x]
        at = pl.multiple_of((2 * x + 1 - core) * piece, piece)
        rows[:, pl.ds(at, piece)] = other_x[x]
    for b, shift in enumerate((0, n_x - 1, 1, 2)):
        copies[2 * b].wait()
        copies[2 * b + 1].wait()
        both = jnp.dot(rows[...], weights[b], preferred_element_type=F32)
        gate, up = both[:, :ff], both[:, ff:]
        at = pl.multiple_of(lax.rem(chip + shift, n_x) * ff, ff)
        hidden[:, pl.ds(at, ff)] = (gate / (1.0 + jnp.exp(-gate)) * up).astype(BF)
    for x in range(n_x):
        out_ref[x] = hidden[...]


def down_kernel(place_ref, hidden_ref, own, prev, nxt, far_a, far_b, keep_ref, send_ref, weights, sems):
    n_x, n_rows, units = hidden_ref.shape
    n_cols, _, width = weights.shape
    ff = units // n_x
    core, chip = place_ref[0], place_ref[1]
    first = far_a.shape[0] - (n_cols // 2) * ff
    start = prev.shape[0] - n_cols * ff
    copies = []
    for b, (shift, piece) in enumerate(((0, own), (n_x - 1, prev), (1, nxt), (2, None))):
        at = pl.multiple_of(lax.rem(chip + shift, n_x) * ff, ff)
        for n in range(n_cols):
            if piece is None:
                part = far_a if n < n_cols // 2 else far_b
                low = first + (n % (n_cols // 2)) * ff
            else:
                part = piece
                low = n * ff + (0 if shift == 0 else start)
            copies.append(
                pltpu.make_async_copy(
                    part.at[low : low + ff], weights.at[n, pl.ds(at, ff)], sems.at[b * n_cols + n]
                )
            )
    for copy in copies:
        copy.start()
    for copy in copies:
        copy.wait()
    mine = n_cols // 2
    rows = hidden_ref[...].reshape(n_x * n_rows, units)
    for ref, side in ((send_ref, 1 - core), (keep_ref, core)):
        for i in range(mine):
            out = jnp.dot(rows, weights[side * mine + i], preferred_element_type=F32).astype(BF)
            for x in range(n_x):
                ref[:, x, :, i * width : (i + 1) * width] = out[
                    x * n_rows : (x + 1) * n_rows
                ].reshape(ref.shape[0], ref.shape[2], width)


def shards(tokens, routes, route_weight, gate_weight, up_weight, down_weight):
    n_x, n_narrow = lax.axis_size("x"), lax.axis_size("narrow")
    n_high, n_low = lax.axis_size("high"), lax.axis_size("low")
    token_count, piece = tokens.shape
    d_model, ff = gate_weight.shape[1:]
    pair = n_high // n_x
    lanes = pair * token_count
    slots = n_narrow * n_low * pair * CAP
    params = pltpu.CompilerParams(vmem_limit_bytes=VMEM)
    smem = pl.BlockSpec(memory_space=pltpu.SMEM)
    vmem = pl.BlockSpec(memory_space=pltpu.VMEM)
    hbm = pl.BlockSpec(memory_space=pl.ANY)
    swap = [(0, 1), (1, 0)]
    up_x = [(i, (i + 1) % n_x) for i in range(n_x)]
    down_x = [(i, (i - 1) % n_x) for i in range(n_x)]

    chip = lax.axis_index("x")
    half, width = d_model // 2, 2 * ff
    n_cols = d_model // n_x // width
    own_g = jnp.concatenate([gate_weight[0], up_weight[0]], axis=1)
    down = (
        down_weight[0]
        .reshape(ff, n_x, n_cols, width)
        .transpose(1, 2, 0, 3)
        .reshape(n_x, n_cols * ff, width)
    )

    def columns_of(shift):
        return lax.dynamic_slice_in_dim(down, lax.rem(chip + shift, n_x), 1, 0)[0]

    beyond = columns_of(2)
    cut = beyond.shape[0] // 2
    own_a, own_b = own_g[:half], own_g[half:]
    prev_a = lax.ppermute(jnp.concatenate([own_a, beyond[:cut]], axis=0), "x", up_x)
    next_b = lax.ppermute(jnp.concatenate([own_b, beyond[cut:]], axis=0), "x", down_x)
    prev_b = lax.ppermute(jnp.concatenate([own_b, columns_of(1)], axis=0), "x", up_x)
    next_a = lax.ppermute(jnp.concatenate([own_a, columns_of(n_x - 1)], axis=0), "x", down_x)

    high = lax.axis_index("high")
    meta = jnp.concatenate([routes.T.astype(BF), route_weight.T.astype(BF)], axis=0)
    meta = jnp.tile(meta, (1, pair))
    mine = jnp.arange(lanes) // token_count == high % pair
    meta = jnp.where(mine[None, :], meta, jnp.zeros_like(meta))
    meta = jnp.pad(meta, ((0, 0), (0, piece - lanes)))
    near = lax.all_gather(
        jnp.concatenate([tokens, meta], axis=0), "high", axis=0, tiled=False
    )
    near, prev_a, next_b = lax.optimization_barrier((near, prev_a, next_b))
    far_a = lax.ppermute(prev_a, "x", up_x)
    far_b = lax.ppermute(next_b, "x", down_x)
    base = (high * n_low).reshape(1).astype(jnp.int32)
    place = jnp.stack([lax.axis_index("core"), chip]).astype(jnp.int32)
    full = near.shape[1]
    rows, weight = pl.pallas_call(
        lambda *refs: select_kernel(n_low, n_high * n_low, *refs),
        grid=(n_x,),
        in_specs=[smem, pl.BlockSpec((pair, full, piece), lambda h: (h, 0, 0))],
        out_specs=[
            pl.BlockSpec((1, slots, piece), lambda h: (h, 0, 0)),
            pl.BlockSpec((1, slots, lanes), lambda h: (h, 0, 0)),
        ],
        out_shape=[
            jax.ShapeDtypeStruct((n_x, slots, piece), BF),
            jax.ShapeDtypeStruct((n_x, slots, lanes), BF),
        ],
        compiler_params=params,
        name="select",
    )(base, near)
    rows, prev_b, next_a = lax.optimization_barrier((rows, prev_b, next_a))
    peers = ("x", "narrow", "low")
    own_x = lax.all_to_all(
        rows.reshape(-1, pair * CAP, piece), peers, split_axis=0, concat_axis=0, tiled=True
    ).reshape(n_x, slots, piece)
    other_x = lax.ppermute(own_x, "core", swap)
    hidden = pl.pallas_call(
        hidden_kernel,
        in_specs=[smem, vmem, vmem] + [hbm] * (2 * n_x),
        out_specs=vmem,
        out_shape=jax.ShapeDtypeStruct((n_x, slots, n_x * ff), BF),
        scratch_shapes=[
            pltpu.VMEM((n_x, d_model, width), BF),
            pltpu.VMEM((slots, d_model), BF),
            pltpu.VMEM((slots, n_x * ff), BF),
            pltpu.SemaphoreType.DMA((2 * n_x,)),
        ],
        compiler_params=params,
        name="hidden",
    )(place, own_x, other_x, own_a, own_b, prev_a, prev_b, next_a, next_b, far_a, far_b)
    hidden = lax.all_to_all(hidden, "x", split_axis=0, concat_axis=0, tiled=True)
    n_near = n_narrow * n_low
    keep, send = pl.pallas_call(
        down_kernel,
        in_specs=[smem, vmem] + [hbm] * 5,
        out_specs=[vmem, vmem],
        out_shape=[jax.ShapeDtypeStruct((n_near, n_x, pair * CAP, piece), BF)] * 2,
        scratch_shapes=[
            pltpu.VMEM((n_cols, n_x * ff, width), BF),
            pltpu.SemaphoreType.DMA((n_x * n_cols,)),
        ],
        compiler_params=params,
        name="down",
    )(place, hidden, columns_of(0), prev_b, next_a, far_a, far_b)
    got = lax.ppermute(send, "core", swap)
    out = (keep.astype(F32) + got.astype(F32)).astype(BF)
    back = lax.all_to_all(
        out.reshape(n_near, -1, piece), ("narrow", "low"), split_axis=0, concat_axis=0, tiled=True
    ).reshape(n_near, n_x, pair * CAP, piece)
    part = pl.pallas_call(
        combine_kernel,
        grid=(n_x,),
        in_specs=[
            pl.BlockSpec((1, slots, lanes), lambda h: (h, 0, 0)),
            pl.BlockSpec((n_near, 1, pair * CAP, piece), lambda h: (0, h, 0, 0)),
        ],
        out_specs=pl.BlockSpec((1, lanes, piece), lambda h: (h, 0, 0)),
        out_shape=jax.ShapeDtypeStruct((n_x, lanes, piece), BF),
        compiler_params=params,
        name="combine",
    )(weight, back)
    part = part.reshape(n_high, token_count, piece)
    up_z = [(i, (i + 1) % n_high) for i in range(n_high)]
    down_z = [(i, (i - 1) % n_high) for i in range(n_high)]

    def mine_for(step):
        block = lax.rem(high + step, n_high)
        return lax.dynamic_slice_in_dim(part, block, 1, 0)[0].astype(F32)

    reach = n_high // 2
    rising = lax.ppermute(mine_for(reach).astype(BF), "high", up_z)
    falling = lax.ppermute(mine_for(reach + 1).astype(BF), "high", down_z)
    for step in range(1, reach):
        rising = (rising.astype(F32) + mine_for(reach - step)).astype(BF)
        rising = lax.ppermute(rising, "high", up_z)
        if step < reach - 1:
            falling = (falling.astype(F32) + mine_for(reach + 1 + step)).astype(BF)
            falling = lax.ppermute(falling, "high", down_z)
    return (mine_for(0) + rising.astype(F32) + falling.astype(F32)).astype(BF)


def solution(mesh):
    sizes = dict(mesh.shape)
    split = Mesh(
        mesh.devices.reshape(
            sizes["shard"] // 2, 2, sizes["narrow"], sizes["wide"] // LOW, LOW
        ),
        ("x", "core", "narrow", "high", "low"),
    )
    group, shard = ("narrow", "high", "low"), ("x", "core")
    placed = (
        P(group, shard),
        P(group, None),
        P(group, None),
        P(group, None, shard),
        P(group, None, shard),
        P(group, shard, None),
    )
    return jax.shard_map(
        shards,
        mesh=split,
        in_specs=placed,
        out_specs=P(group, shard),
        check_vma=False,
    )
```

```python
import jax
import jax.numpy as jnp
from jax import lax
from jax.experimental import pallas as pl
from jax.experimental.pallas import tpu as pltpu
from jax.sharding import Mesh, PartitionSpec as P

BF = jnp.bfloat16
F32 = jnp.float32
CAP = 8
LOW = 4
VMEM = 56 << 20


def select_kernel(n_low, wide_count, base_ref, x_ref, rows_ref, weight_ref):
    pair, full, _ = x_ref.shape
    slots, lanes = weight_ref.shape[1:]
    tokens = lanes // pair
    top = (full - tokens) // 2
    meta = x_ref[0, tokens:, :lanes].astype(F32)
    for i in range(1, pair):
        meta += x_ref[i, tokens:, :lanes].astype(F32)
    row = lax.broadcasted_iota(jnp.int32, (slots, lanes), 0)
    lane = lax.broadcasted_iota(jnp.int32, (slots, lanes), 1)
    slot = row % CAP
    place = row // (CAP * pair)
    expert = ((place // n_low) * wide_count + place % n_low + base_ref[0]).astype(F32)
    expert = jnp.where(lane // tokens == (row // CAP) % pair, expert, -1.0)
    hit = jnp.zeros((slots, lanes), F32)
    weight = jnp.zeros((slots, lanes), F32)
    for k in range(top):
        same = meta[k : k + 1, :] == expert
        hit = jnp.where(same, 1.0, hit)
        weight = jnp.where(same, meta[top + k : top + k + 1, :], weight)
    earlier = (
        lax.broadcasted_iota(jnp.int32, (lanes, lanes), 0)
        < lax.broadcasted_iota(jnp.int32, (lanes, lanes), 1)
    ).astype(BF)
    rank = jnp.dot(hit.astype(BF), earlier, preferred_element_type=F32)
    first = rank == slot.astype(F32)
    chosen = jnp.where(first, hit, 0.0).astype(BF)
    weight_ref[0] = jnp.where(first, weight, 0.0).astype(BF)
    both = jnp.concatenate([x_ref[i, :tokens, :] for i in range(pair)], axis=0)
    rows_ref[0] = jnp.dot(chosen, both, preferred_element_type=F32).astype(BF)


def combine_kernel(weight_ref, back_ref, part_ref):
    part_ref[0] = lax.dot_general(
        weight_ref[0], back_ref[0], (((0,), (0,)), ((), ())), preferred_element_type=F32
    ).astype(BF)


def expert_work(core_ref, own_x, other_x, parts, weights, rows, hidden, sems):
    n_x, _, piece = own_x.shape
    d_model = rows.shape[1]
    blocks, _, width = weights.shape
    ff = width // 2
    half = parts[0].shape[0]
    core = core_ref[0]
    copies = [
        pltpu.make_async_copy(
            part, weights.at[i // 2, (i % 2) * half : (i % 2 + 1) * half], sems.at[i]
        )
        for i, part in enumerate(parts)
    ]
    for copy in copies:
        copy.start()
    for x in range(n_x):
        at = pl.multiple_of((2 * x + core) * piece, piece)
        rows[:, pl.ds(at, piece)] = own_x[x]
        at = pl.multiple_of((2 * x + 1 - core) * piece, piece)
        rows[:, pl.ds(at, piece)] = other_x[x]
    for b in range(blocks):
        copies[2 * b].wait()
        copies[2 * b + 1].wait()
        both = jnp.dot(rows[...], weights[b, :d_model, :], preferred_element_type=F32)
        gate, up = both[:, :ff], both[:, ff:]
        hidden[:, b * ff : (b + 1) * ff] = (gate / (1.0 + jnp.exp(-gate)) * up).astype(BF)
    for n in range(d_model // width):
        at = d_model + n * ff
        down = jnp.concatenate([weights[b, at : at + ff, :] for b in range(blocks)], axis=0)
        yield slice(n * width, (n + 1) * width), jnp.dot(
            hidden[...], down, preferred_element_type=F32
        )


def near_kernel(core_ref, own_x, other_x, *refs):
    parts, (total_ref, weights, rows, hidden, sems) = refs[:-5], refs[-5:]
    for at, term in expert_work(core_ref, own_x, other_x, parts, weights, rows, hidden, sems):
        total_ref[:, at] = term


def far_kernel(core_ref, own_x, other_x, near_ref, *refs):
    parts, (keep_ref, send_ref, weights, rows, hidden, total, sems) = refs[:-7], refs[-7:]
    n_x, _, piece = own_x.shape
    core = core_ref[0]
    for at, term in expert_work(core_ref, own_x, other_x, parts, weights, rows, hidden, sems):
        total[:, at] = (near_ref[:, at] + term).astype(BF)
    for x in range(n_x):
        at = pl.multiple_of((2 * x + core) * piece, piece)
        keep_ref[x] = total[:, pl.ds(at, piece)]
        at = pl.multiple_of((2 * x + 1 - core) * piece, piece)
        send_ref[x] = total[:, pl.ds(at, piece)]


def shards(tokens, routes, route_weight, gate_weight, up_weight, down_weight):
    n_x, n_narrow = lax.axis_size("x"), lax.axis_size("narrow")
    n_high, n_low = lax.axis_size("high"), lax.axis_size("low")
    token_count, piece = tokens.shape
    d_model, ff = gate_weight.shape[1:]
    pair = n_high // n_x
    lanes = pair * token_count
    slots = n_narrow * n_low * pair * CAP
    params = pltpu.CompilerParams(vmem_limit_bytes=VMEM)
    smem = pl.BlockSpec(memory_space=pltpu.SMEM)
    vmem = pl.BlockSpec(memory_space=pltpu.VMEM)
    hbm = pl.BlockSpec(memory_space=pl.ANY)
    swap = [(0, 1), (1, 0)]
    up_x = [(i, (i + 1) % n_x) for i in range(n_x)]
    down_x = [(i, (i - 1) % n_x) for i in range(n_x)]

    own_w = jnp.concatenate(
        [
            jnp.concatenate([gate_weight[0], up_weight[0]], axis=1),
            down_weight[0]
            .reshape(ff, d_model // (2 * ff), 2 * ff)
            .transpose(1, 0, 2)
            .reshape(d_model // 2, 2 * ff),
        ],
        axis=0,
    )
    half = own_w.shape[0] // 2
    own_a, own_b = own_w[:half], own_w[half:]
    prev_a = lax.ppermute(own_a, "x", up_x)
    next_b = lax.ppermute(own_b, "x", down_x)
    prev_b = lax.ppermute(own_b, "x", up_x)
    next_a = lax.ppermute(own_a, "x", down_x)

    high = lax.axis_index("high")
    meta = jnp.concatenate([routes.T.astype(BF), route_weight.T.astype(BF)], axis=0)
    meta = jnp.tile(meta, (1, pair))
    mine = jnp.arange(lanes) // token_count == high % pair
    meta = jnp.where(mine[None, :], meta, jnp.zeros_like(meta))
    meta = jnp.pad(meta, ((0, 0), (0, piece - lanes)))
    near = lax.all_gather(
        jnp.concatenate([tokens, meta], axis=0), "high", axis=0, tiled=False
    )
    near, prev_a, next_b = lax.optimization_barrier((near, prev_a, next_b))
    far_a = lax.ppermute(prev_a, "x", up_x)
    far_b = lax.ppermute(next_b, "x", down_x)
    base = (high * n_low).reshape(1).astype(jnp.int32)
    core = lax.axis_index("core").reshape(1).astype(jnp.int32)
    full = near.shape[1]
    rows, weight = pl.pallas_call(
        lambda *refs: select_kernel(n_low, n_high * n_low, *refs),
        grid=(n_x,),
        in_specs=[smem, pl.BlockSpec((pair, full, piece), lambda h: (h, 0, 0))],
        out_specs=[
            pl.BlockSpec((1, slots, piece), lambda h: (h, 0, 0)),
            pl.BlockSpec((1, slots, lanes), lambda h: (h, 0, 0)),
        ],
        out_shape=[
            jax.ShapeDtypeStruct((n_x, slots, piece), BF),
            jax.ShapeDtypeStruct((n_x, slots, lanes), BF),
        ],
        compiler_params=params,
        name="select",
    )(base, near)
    rows, prev_b, next_a = lax.optimization_barrier((rows, prev_b, next_a))
    peers = ("x", "narrow", "low")
    own_x = lax.all_to_all(
        rows.reshape(-1, pair * CAP, piece), peers, split_axis=0, concat_axis=0, tiled=True
    ).reshape(n_x, slots, piece)
    other_x = lax.ppermute(own_x, "core", swap)
    def scratch(blocks):
        return [
            pltpu.VMEM((blocks,) + own_w.shape, BF),
            pltpu.VMEM((slots, d_model), BF),
            pltpu.VMEM((slots, blocks * ff), BF),
        ]

    near_sum = pl.pallas_call(
        near_kernel,
        in_specs=[smem, vmem, vmem] + [hbm] * 6,
        out_specs=vmem,
        out_shape=jax.ShapeDtypeStruct((slots, d_model), F32),
        scratch_shapes=scratch(3) + [pltpu.SemaphoreType.DMA((6,))],
        compiler_params=params,
        name="near",
    )(core, own_x, other_x, own_a, own_b, prev_a, prev_b, next_a, next_b)
    keep, send = pl.pallas_call(
        far_kernel,
        in_specs=[smem, vmem, vmem, vmem] + [hbm] * 2,
        out_specs=[vmem, vmem],
        out_shape=[jax.ShapeDtypeStruct(own_x.shape, BF)] * 2,
        scratch_shapes=scratch(1)
        + [pltpu.VMEM((slots, d_model), BF), pltpu.SemaphoreType.DMA((2,))],
        compiler_params=params,
        name="far",
    )(core, own_x, other_x, near_sum, far_a, far_b)
    got = lax.ppermute(send, "core", swap)
    out = (keep.astype(F32) + got.astype(F32)).astype(BF)
    back = lax.all_to_all(
        out.reshape(-1, pair * CAP, piece), peers, split_axis=0, concat_axis=0, tiled=True
    ).reshape(n_x, slots, piece)
    part = pl.pallas_call(
        combine_kernel,
        grid=(n_x,),
        in_specs=[
            pl.BlockSpec((1, slots, lanes), lambda h: (h, 0, 0)),
            pl.BlockSpec((1, slots, piece), lambda h: (h, 0, 0)),
        ],
        out_specs=pl.BlockSpec((1, lanes, piece), lambda h: (h, 0, 0)),
        out_shape=jax.ShapeDtypeStruct((n_x, lanes, piece), BF),
        compiler_params=params,
        name="combine",
    )(weight, back)
    part = part.reshape(n_high, token_count, piece)
    up_z = [(i, (i + 1) % n_high) for i in range(n_high)]
    down_z = [(i, (i - 1) % n_high) for i in range(n_high)]

    def mine_for(step):
        block = lax.rem(high + step, n_high)
        return lax.dynamic_slice_in_dim(part, block, 1, 0)[0].astype(F32)

    reach = n_high // 2
    rising = lax.ppermute(mine_for(reach).astype(BF), "high", up_z)
    falling = lax.ppermute(mine_for(reach + 1).astype(BF), "high", down_z)
    for step in range(1, reach):
        rising = (rising.astype(F32) + mine_for(reach - step)).astype(BF)
        rising = lax.ppermute(rising, "high", up_z)
        if step < reach - 1:
            falling = (falling.astype(F32) + mine_for(reach + 1 + step)).astype(BF)
            falling = lax.ppermute(falling, "high", down_z)
    return (mine_for(0) + rising.astype(F32) + falling.astype(F32)).astype(BF)


def solution(mesh):
    sizes = dict(mesh.shape)
    split = Mesh(
        mesh.devices.reshape(
            sizes["shard"] // 2, 2, sizes["narrow"], sizes["wide"] // LOW, LOW
        ),
        ("x", "core", "narrow", "high", "low"),
    )
    group, shard = ("narrow", "high", "low"), ("x", "core")
    placed = (
        P(group, shard),
        P(group, None),
        P(group, None),
        P(group, None, shard),
        P(group, None, shard),
        P(group, shard, None),
    )
    return jax.shard_map(
        shards,
        mesh=split,
        in_specs=placed,
        out_specs=P(group, shard),
        check_vma=False,
    )
```

```python
import jax
import jax.numpy as jnp
from jax import lax
from jax.experimental import pallas as pl
from jax.experimental.pallas import tpu as pltpu
from jax.sharding import Mesh, PartitionSpec as P

BF = jnp.bfloat16
F32 = jnp.float32
CAP = 8
LOW = 4
VMEM = 56 << 20


def select_kernel(n_low, wide_count, base_ref, x_ref, rows_ref, weight_ref):
    pair, full, _ = x_ref.shape
    slots, lanes = weight_ref.shape[1:]
    tokens = lanes // pair
    top = (full - tokens) // 2
    meta = x_ref[0, tokens:, :lanes].astype(F32)
    for i in range(1, pair):
        meta += x_ref[i, tokens:, :lanes].astype(F32)
    row = lax.broadcasted_iota(jnp.int32, (slots, lanes), 0)
    lane = lax.broadcasted_iota(jnp.int32, (slots, lanes), 1)
    slot = row % CAP
    place = row // (CAP * pair)
    expert = ((place // n_low) * wide_count + place % n_low + base_ref[0]).astype(F32)
    expert = jnp.where(lane // tokens == (row // CAP) % pair, expert, -1.0)
    hit = jnp.zeros((slots, lanes), F32)
    weight = jnp.zeros((slots, lanes), F32)
    for k in range(top):
        same = meta[k : k + 1, :] == expert
        hit = jnp.where(same, 1.0, hit)
        weight = jnp.where(same, meta[top + k : top + k + 1, :], weight)
    earlier = (
        lax.broadcasted_iota(jnp.int32, (lanes, lanes), 0)
        < lax.broadcasted_iota(jnp.int32, (lanes, lanes), 1)
    ).astype(BF)
    rank = jnp.dot(hit.astype(BF), earlier, preferred_element_type=F32)
    first = rank == slot.astype(F32)
    chosen = jnp.where(first, hit, 0.0).astype(BF)
    weight_ref[0] = jnp.where(first, weight, 0.0).astype(BF)
    both = jnp.concatenate([x_ref[i, :tokens, :] for i in range(pair)], axis=0)
    rows_ref[0] = jnp.dot(chosen, both, preferred_element_type=F32).astype(BF)


def combine_kernel(weight_ref, back_ref, part_ref):
    part_ref[0] = lax.dot_general(
        weight_ref[0], back_ref[0], (((0,), (0,)), ((), ())), preferred_element_type=F32
    ).astype(BF)


def expert_work(core_ref, own_x, other_x, parts, weights, rows, hidden, sems):
    n_x, _, piece = own_x.shape
    d_model = rows.shape[1]
    blocks, _, width = weights.shape
    ff = width // 2
    half = parts[0].shape[0]
    core = core_ref[0]
    copies = [
        pltpu.make_async_copy(
            part, weights.at[i // 2, (i % 2) * half : (i % 2 + 1) * half], sems.at[i]
        )
        for i, part in enumerate(parts)
    ]
    for copy in copies:
        copy.start()
    for x in range(n_x):
        at = pl.multiple_of((2 * x + core) * piece, piece)
        rows[:, pl.ds(at, piece)] = own_x[x]
        at = pl.multiple_of((2 * x + 1 - core) * piece, piece)
        rows[:, pl.ds(at, piece)] = other_x[x]
    for b in range(blocks):
        copies[2 * b].wait()
        copies[2 * b + 1].wait()
        both = jnp.dot(rows[...], weights[b, :d_model, :], preferred_element_type=F32)
        gate, up = both[:, :ff], both[:, ff:]
        hidden[:, b * ff : (b + 1) * ff] = (gate / (1.0 + jnp.exp(-gate)) * up).astype(BF)
    for n in range(d_model // width):
        at = d_model + n * ff
        down = jnp.concatenate([weights[b, at : at + ff, :] for b in range(blocks)], axis=0)
        yield slice(n * width, (n + 1) * width), jnp.dot(
            hidden[...], down, preferred_element_type=F32
        )


def near_kernel(core_ref, own_x, other_x, *refs):
    parts, (total_ref, weights, rows, hidden, sems) = refs[:-5], refs[-5:]
    for at, term in expert_work(core_ref, own_x, other_x, parts, weights, rows, hidden, sems):
        total_ref[:, at] = term.astype(BF)


def far_kernel(core_ref, own_x, other_x, near_ref, *refs):
    parts, (keep_ref, send_ref, weights, rows, hidden, total, sems) = refs[:-7], refs[-7:]
    n_x, _, piece = own_x.shape
    core = core_ref[0]
    for at, term in expert_work(core_ref, own_x, other_x, parts, weights, rows, hidden, sems):
        total[:, at] = (near_ref[:, at].astype(F32) + term).astype(BF)
    for x in range(n_x):
        at = pl.multiple_of((2 * x + core) * piece, piece)
        keep_ref[x] = total[:, pl.ds(at, piece)]
        at = pl.multiple_of((2 * x + 1 - core) * piece, piece)
        send_ref[x] = total[:, pl.ds(at, piece)]


def shards(tokens, routes, route_weight, gate_weight, up_weight, down_weight):
    n_x, n_narrow = lax.axis_size("x"), lax.axis_size("narrow")
    n_high, n_low = lax.axis_size("high"), lax.axis_size("low")
    token_count, piece = tokens.shape
    d_model, ff = gate_weight.shape[1:]
    pair = n_high // n_x
    lanes = pair * token_count
    slots = n_narrow * n_low * pair * CAP
    params = pltpu.CompilerParams(vmem_limit_bytes=VMEM)
    smem = pl.BlockSpec(memory_space=pltpu.SMEM)
    vmem = pl.BlockSpec(memory_space=pltpu.VMEM)
    hbm = pl.BlockSpec(memory_space=pl.ANY)
    swap = [(0, 1), (1, 0)]
    up_x = [(i, (i + 1) % n_x) for i in range(n_x)]
    down_x = [(i, (i - 1) % n_x) for i in range(n_x)]

    width = 2 * ff
    half = (d_model + d_model // 2) // 2
    gate, up = gate_weight[0], up_weight[0]
    own_a = jnp.concatenate([gate[:half], up[:half]], axis=1)
    own_b = jnp.concatenate(
        [
            jnp.concatenate([gate[half:], up[half:]], axis=1),
            down_weight[0]
            .reshape(ff, d_model // width, width)
            .transpose(1, 0, 2)
            .reshape(d_model // 2, width),
        ],
        axis=0,
    )
    prev_a = lax.ppermute(own_a, "x", up_x)
    next_b = lax.ppermute(own_b, "x", down_x)
    prev_b = lax.ppermute(own_b, "x", up_x)
    next_a = lax.ppermute(own_a, "x", down_x)

    high = lax.axis_index("high")
    meta = jnp.concatenate([routes.T.astype(BF), route_weight.T.astype(BF)], axis=0)
    meta = jnp.tile(meta, (1, pair))
    mine = jnp.arange(lanes) // token_count == high % pair
    meta = jnp.where(mine[None, :], meta, jnp.zeros_like(meta))
    meta = jnp.pad(meta, ((0, 0), (0, piece - lanes)))
    near = lax.all_gather(
        jnp.concatenate([tokens, meta], axis=0), "high", axis=0, tiled=False
    )
    near, prev_a, next_b = lax.optimization_barrier((near, prev_a, next_b))
    far_a = lax.ppermute(prev_a, "x", up_x)
    far_b = lax.ppermute(next_b, "x", down_x)
    base = (high * n_low).reshape(1).astype(jnp.int32)
    core = lax.axis_index("core").reshape(1).astype(jnp.int32)
    full = near.shape[1]
    rows, weight = pl.pallas_call(
        lambda *refs: select_kernel(n_low, n_high * n_low, *refs),
        grid=(n_x,),
        in_specs=[smem, pl.BlockSpec((pair, full, piece), lambda h: (h, 0, 0))],
        out_specs=[
            pl.BlockSpec((1, slots, piece), lambda h: (h, 0, 0)),
            pl.BlockSpec((1, slots, lanes), lambda h: (h, 0, 0)),
        ],
        out_shape=[
            jax.ShapeDtypeStruct((n_x, slots, piece), BF),
            jax.ShapeDtypeStruct((n_x, slots, lanes), BF),
        ],
        compiler_params=params,
        name="select",
    )(base, near)
    rows, prev_b, next_a = lax.optimization_barrier((rows, prev_b, next_a))
    peers = ("x", "narrow", "low")
    own_x = lax.all_to_all(
        rows.reshape(-1, pair * CAP, piece), peers, split_axis=0, concat_axis=0, tiled=True
    ).reshape(n_x, slots, piece)
    other_x = lax.ppermute(own_x, "core", swap)
    def scratch(blocks):
        return [
            pltpu.VMEM((blocks, 2 * half, width), BF),
            pltpu.VMEM((slots, d_model), BF),
            pltpu.VMEM((slots, blocks * ff), BF),
        ]

    near_sum = pl.pallas_call(
        near_kernel,
        in_specs=[smem, vmem, vmem] + [hbm] * 6,
        out_specs=vmem,
        out_shape=jax.ShapeDtypeStruct((slots, d_model), BF),
        scratch_shapes=scratch(3) + [pltpu.SemaphoreType.DMA((6,))],
        compiler_params=params,
        name="near",
    )(core, own_x, other_x, own_a, own_b, prev_a, prev_b, next_a, next_b)
    keep, send = pl.pallas_call(
        far_kernel,
        in_specs=[smem, vmem, vmem, vmem] + [hbm] * 2,
        out_specs=[vmem, vmem],
        out_shape=[jax.ShapeDtypeStruct(own_x.shape, BF)] * 2,
        scratch_shapes=scratch(1)
        + [pltpu.VMEM((slots, d_model), BF), pltpu.SemaphoreType.DMA((2,))],
        compiler_params=params,
        name="far",
    )(core, own_x, other_x, near_sum, far_a, far_b)
    got = lax.ppermute(send, "core", swap)
    out = (keep.astype(F32) + got.astype(F32)).astype(BF)
    back = lax.all_to_all(
        out.reshape(-1, pair * CAP, piece), peers, split_axis=0, concat_axis=0, tiled=True
    ).reshape(n_x, slots, piece)
    part = pl.pallas_call(
        combine_kernel,
        grid=(n_x,),
        in_specs=[
            pl.BlockSpec((1, slots, lanes), lambda h: (h, 0, 0)),
            pl.BlockSpec((1, slots, piece), lambda h: (h, 0, 0)),
        ],
        out_specs=pl.BlockSpec((1, lanes, piece), lambda h: (h, 0, 0)),
        out_shape=jax.ShapeDtypeStruct((n_x, lanes, piece), BF),
        compiler_params=params,
        name="combine",
    )(weight, back)
    part = part.reshape(n_high, token_count, piece)
    up_z = [(i, (i + 1) % n_high) for i in range(n_high)]
    down_z = [(i, (i - 1) % n_high) for i in range(n_high)]

    def mine_for(step):
        block = lax.rem(high + step, n_high)
        return lax.dynamic_slice_in_dim(part, block, 1, 0)[0].astype(F32)

    reach = n_high // 2
    rising = lax.ppermute(mine_for(reach).astype(BF), "high", up_z)
    falling = lax.ppermute(mine_for(reach + 1).astype(BF), "high", down_z)
    for step in range(1, reach):
        rising = (rising.astype(F32) + mine_for(reach - step)).astype(BF)
        rising = lax.ppermute(rising, "high", up_z)
        if step < reach - 1:
            falling = (falling.astype(F32) + mine_for(reach + 1 + step)).astype(BF)
            falling = lax.ppermute(falling, "high", down_z)
    return (mine_for(0) + rising.astype(F32) + falling.astype(F32)).astype(BF)


def solution(mesh):
    sizes = dict(mesh.shape)
    split = Mesh(
        mesh.devices.reshape(
            sizes["shard"] // 2, 2, sizes["narrow"], sizes["wide"] // LOW, LOW
        ),
        ("x", "core", "narrow", "high", "low"),
    )
    group, shard = ("narrow", "high", "low"), ("x", "core")
    placed = (
        P(group, shard),
        P(group, None),
        P(group, None),
        P(group, None, shard),
        P(group, None, shard),
        P(group, shard, None),
    )
    return jax.shard_map(
        shards,
        mesh=split,
        in_specs=placed,
        out_specs=P(group, shard),
        check_vma=False,
    )
```
